1024 devices in a mesh: row: 64 (over y_hi, x, core), col: 16 (over z, y_lo).
Axes of the slice: x: 8, y: 8 (y_hi: 4, y_lo: 2; y = y_hi * 2 + y_lo), z: 8, core: 2. Of those that a mesh axis runs over, the one named last changes fastest.
Arguments:
- picture_vectors: bfloat16 [16384, 1152], P(('row', 'col')), may hold values from -50 to 50
- caption_vectors: bfloat16 [16384, 1152], P(('row', 'col')), may hold values from -50 to 50
- caption_partner_position: int32 [16384], replicated, may hold values from 0 to 16383, as said below
- sharpness_factor: float32 [1], replicated, may hold values from 9 to 12
- affine_offset_array: float32 [1], replicated, may hold values from -10 to -7
Outputs:
- image_grad: float32 [16384, 1152], P(('row', 'col'))
- text_grad: float32 [16384, 1152], P(('row', 'col'))
- loss_rows: float32 [16384], P(('row', 'col'))
The draws below stay inside these ranges and needn't reach their ends.
Inputs may be any that keep to these rules, and one draw needn't show every extreme that they name: `caption_partner_position`: each text index appears exactly once.
All inputs are finite; a program needn't handle non-finite values.
Results may differ from the reference program's by a relative error of at most 0.0023.
Values may be sent and summed in bfloat16 or wider, within the bound.
No kernel may reach another device: no remote copies, remote signals or barrier semaphores. Data moves between devices by JAX's collectives and lax.ppermute only.
A program may use at most 32 MiB of HBM per device.

```python
import jax
import jax.numpy as jnp
from jax import lax

D = 1152
PAIRS_PER_CHIP = 16
TOTAL = 16384
N_ROW = 64
N_COL = 16


def pair_order(key):
    return jax.random.permutation(jax.random.fold_in(key, 11), TOTAL).astype(jnp.int32)


def common_example_entries(key):
    groups = max(TOTAL // 32, 1)
    member = jax.random.randint(jax.random.fold_in(key, 12), (TOTAL,), 0, groups)
    strength = jax.random.uniform(jax.random.fold_in(key, 14), (groups,), jnp.float32, 0.9, 1.6)
    centers = jnp.clip(jax.random.normal(jax.random.fold_in(key, 15), (groups, D), jnp.float32), -5.0, 5.0)
    private = jnp.clip(jax.random.normal(jax.random.fold_in(key, 16), (TOTAL, D), jnp.float32), -5.0, 5.0)
    return strength[member][:, None] * centers[member] + 0.7 * private


def draw_caption_partner_position(key, part):
    return pair_order(key)


def draw_picture_vectors(key, part):
    shared = common_example_entries(key)
    key = jax.random.fold_in(key, 1)
    rows = shared + 0.5 * jnp.clip(jax.random.normal(key, (TOTAL, D), jnp.float32), -5.0, 5.0)
    return rows.astype(jnp.bfloat16)


def draw_caption_vectors(key, part):
    shared = common_example_entries(key)
    order = pair_order(key)
    key = jax.random.fold_in(key, 3)
    noise = 0.5 * jnp.clip(jax.random.normal(key, (TOTAL, D), jnp.float32), -5.0, 5.0)
    rows = jnp.zeros((TOTAL, D), jnp.float32).at[order].set(shared + noise)
    return rows.astype(jnp.bfloat16)


def setup_inputs(seed: int = 0) -> dict:
    key_of = jax.random.split(jax.random.key(seed), 6)
    return {
        "picture_vectors": draw_picture_vectors(jax.random.fold_in(key_of[5], 71), 0),
        "caption_vectors": draw_caption_vectors(jax.random.fold_in(key_of[5], 71), 0),
        "caption_partner_position": draw_caption_partner_position(jax.random.fold_in(key_of[5], 71), 0),
        "sharpness_factor": jnp.clip(jax.random.uniform(key_of[3], (1,), jnp.float32, 9.0, 12.0), 9.0, 12.0),
        "affine_offset_array": jnp.clip(jax.random.uniform(key_of[4], (1,), jnp.float32, -10.0, -7.0), -10.0, -7.0),
    }


def normalize(raw):
    values = raw.astype(jnp.float32)
    return values * lax.rsqrt(lax.optimization_barrier(jnp.sum(values * values, axis=1, keepdims=True)) + 1e-06)

def reference(picture_vectors, caption_vectors, caption_partner_position, sharpness_factor, affine_offset_array):
    total = picture_vectors.shape[0]
    width = picture_vectors.shape[1]
    block = PAIRS_PER_CHIP * N_COL
    img_half = normalize(picture_vectors).astype(jnp.bfloat16)
    text_half_split = normalize(caption_vectors).astype(jnp.bfloat16)
    similarity_multiplier = sharpness_factor[0]
    shift = affine_offset_array[0]
    text_ids = jnp.arange(total, dtype=jnp.int32)

    def step(carry, index):
        start = (index * block).astype(jnp.int32)
        rows = lax.dynamic_slice_in_dim(img_half, start, block, 0)
        pairs = lax.dynamic_slice_in_dim(caption_partner_position, start, block, 0)
        logits = similarity_multiplier * jnp.dot(rows, text_half_split.T, preferred_element_type=jnp.float32) + shift
        positive = (pairs[:, None] == text_ids[None, :]).astype(jnp.float32)
        sign = 2.0 * positive - 1.0
        losses = lax.optimization_barrier(jnp.sum(jax.nn.softplus(-sign * logits), axis=1))
        slope = (jax.nn.sigmoid(logits) - positive).astype(jnp.bfloat16)
        img_dir = similarity_multiplier * jnp.dot(slope, text_half_split, preferred_element_type=jnp.float32)
        carry = carry + similarity_multiplier * jnp.dot(slope.T, rows, preferred_element_type=jnp.float32)
        return (carry, (img_dir, losses))
    initial_carry = jnp.zeros((total, width), jnp.float32)
    txt_dir, outputs = lax.scan(step, initial_carry, jnp.arange(N_ROW, dtype=jnp.int32))
    img_dir = outputs[0].reshape(total, width)
    loss_rows = outputs[1].reshape(total)
    unused, image_back = jax.vjp(normalize, picture_vectors.astype(jnp.float32))
    unused2, text_backward = jax.vjp(normalize, caption_vectors.astype(jnp.float32))
    return (image_back(img_dir)[0], text_backward(txt_dir)[0], loss_rows)
```

```python
import jax
import jax.numpy as jnp
from jax import lax
from jax.sharding import Mesh, PartitionSpec as P

FINE = ("yhi", "x", "core", "z", "ylo")
FINE_SIZES = (4, 8, 2, 8, 2)
IMAGE_GROUP = ("core", "z", "ylo")
TEXT_GROUP = ("yhi", "x")
SEND_SCALE = 32.0


def normalize(raw):
    values = raw.astype(jnp.float32)
    return values * lax.rsqrt(jnp.sum(values * values, axis=1, keepdims=True) + 1e-06)


def gather(block, axes):
    copies = jnp.broadcast_to(block[None], (lax.axis_size(axes),) + block.shape)
    return lax.all_to_all(copies, axes, 0, 0, tiled=True)


def scatter(parts, axes):
    count = lax.axis_size(axes)
    return lax.all_to_all(
        parts.reshape(count, parts.shape[0] // count, parts.shape[1]), axes, 0, 0, tiled=True
    )


def per_device(
    picture_vectors,
    caption_vectors,
    caption_partner_position,
    sharpness_factor,
    affine_offset_array,
):
    own_rows, width = picture_vectors.shape
    image_devices = lax.axis_size(IMAGE_GROUP)
    text_devices = lax.axis_size(TEXT_GROUP)
    similarity_multiplier = sharpness_factor[0]
    shift = affine_offset_array[0]
    txt_block = gather(normalize(caption_vectors).astype(jnp.bfloat16), TEXT_GROUP).reshape(-1, width)
    img_block = gather(normalize(picture_vectors).astype(jnp.bfloat16), IMAGE_GROUP).reshape(-1, width)
    group_rows = own_rows * image_devices
    my_pairs = lax.dynamic_slice_in_dim(
        caption_partner_position, lax.axis_index(TEXT_GROUP) * group_rows, group_rows, 0
    )
    column = jnp.arange(own_rows * text_devices, dtype=jnp.int32)
    text_ids = (
        column // own_rows * group_rows + lax.axis_index(IMAGE_GROUP) * own_rows + column % own_rows
    )
    logits = (
        similarity_multiplier
        * lax.dot_general(
            img_block, txt_block, (((1,), (1,)), ((), ())), preferred_element_type=jnp.float32
        )
        + shift
    )
    positive = (my_pairs[:, None] == text_ids[None, :]).astype(jnp.float32)
    sign = 2.0 * positive - 1.0
    partial_loss = jnp.sum(jax.nn.softplus(-sign * logits), axis=1)
    slope = (jax.nn.sigmoid(logits) - positive).astype(jnp.bfloat16)
    txt_part = lax.dot_general(
        slope, img_block, (((0,), (0,)), ((), ())), preferred_element_type=jnp.float32
    )
    txt_terms = scatter((SEND_SCALE * txt_part).astype(jnp.float16), TEXT_GROUP)
    img_part = jnp.dot(slope, txt_block, preferred_element_type=jnp.float32)
    loss_high = partial_loss.astype(jnp.float16)
    loss_low = (partial_loss - loss_high.astype(jnp.float32)).astype(jnp.float16)
    lane = jnp.arange(128)[None, :]
    losses = jnp.where(lane == 0, loss_high[:, None], jnp.where(lane == 1, loss_low[:, None], 0))
    img_terms = scatter(
        jnp.concatenate([(SEND_SCALE * img_part).astype(jnp.float16), losses], axis=1), IMAGE_GROUP
    )
    img_sum = jnp.sum(img_terms.astype(jnp.float32), axis=0)
    img_dir = (similarity_multiplier / SEND_SCALE) * img_sum[:, :width]
    loss_rows = img_sum[:, width] + img_sum[:, width + 1]
    txt_dir = (similarity_multiplier / SEND_SCALE) * jnp.sum(txt_terms.astype(jnp.float32), axis=0)
    unused, image_back = jax.vjp(normalize, picture_vectors.astype(jnp.float32))
    unused2, text_backward = jax.vjp(normalize, caption_vectors.astype(jnp.float32))
    return (image_back(img_dir)[0], text_backward(txt_dir)[0], loss_rows)


def solution(mesh):
    fine = Mesh(mesh.devices.reshape(FINE_SIZES), FINE)
    in_specs = (P(FINE, None), P(FINE, None), P(), P(), P())
    out_specs = (P(FINE, None), P(FINE, None), P(FINE))
    return jax.shard_map(
        per_device, mesh=fine, in_specs=in_specs, out_specs=out_specs, check_vma=False
    )
```

```python
import jax
import jax.numpy as jnp
from jax import lax
from jax.sharding import Mesh, PartitionSpec as P

FINE = ("y2", "y1", "x", "core", "z2", "z1", "z0", "y0")
FINE_SIZES = (2, 2, 8, 2, 2, 2, 2, 2)
IMAGE_GROUP = ("core", "z2", "z1", "z0", "y2")
TEXT_GROUP = ("y1", "x", "y0")
SEND_SCALE = 2.0
LOSS_SCALE = 0.125


def normalize(raw):
    values = raw.astype(jnp.float32)
    return values * lax.rsqrt(jnp.sum(values * values, axis=1, keepdims=True) + 1e-06)


def gather(block, axes):
    copies = jnp.broadcast_to(block[None], (lax.axis_size(axes),) + block.shape)
    return lax.all_to_all(copies, axes, 0, 0, tiled=True)


def scatter(parts, axes):
    count = lax.axis_size(axes)
    return lax.all_to_all(
        parts.reshape(count, parts.shape[0] // count, parts.shape[1]), axes, 0, 0, tiled=True
    )


def halve(total, axis, place, tie=None):
    mine = lax.axis_index(axis)
    sent = lax.dynamic_index_in_dim(total, 1 - mine, place, keepdims=False).astype(jnp.float16)
    if tie is not None:
        sent = sent + jnp.minimum(jnp.abs(tie), 0).astype(jnp.float16)
    came = lax.ppermute(sent, axis, [(0, 1), (1, 0)])
    return lax.dynamic_index_in_dim(total, mine, place, keepdims=False) + came.astype(jnp.float32)


def per_device(
    picture_vectors,
    caption_vectors,
    caption_partner_position,
    sharpness_factor,
    affine_offset_array,
):
    own_rows, width = picture_vectors.shape
    similarity_multiplier = sharpness_factor[0]
    shift = affine_offset_array[0]
    txt_block = gather(normalize(caption_vectors).astype(jnp.bfloat16), TEXT_GROUP).reshape(-1, width)
    img_block = normalize(picture_vectors).astype(jnp.bfloat16)
    for axes in (("y2",), ("z2", "z1", "z0")):
        img_block = lax.all_gather(img_block, axes, axis=0, tiled=True)
    img_block = jnp.concatenate([img_block, lax.ppermute(img_block, "core", [(0, 1), (1, 0)])])
    ids = jnp.arange(caption_partner_position.shape[0], dtype=jnp.int32)

    def of_group(array, group):
        rows = array.reshape(FINE_SIZES + (own_rows,))
        for place, axis in enumerate(FINE):
            if axis not in group:
                rows = lax.dynamic_slice_in_dim(rows, lax.axis_index(axis), 1, place)
        order = [FINE.index(axis) for axis in group]
        order = order + [i for i in range(len(FINE) + 1) if i not in order]
        return rows.transpose(order).reshape(-1)

    my_pairs = of_group(caption_partner_position, IMAGE_GROUP)
    half = my_pairs.shape[0] // 2
    my_pairs = lax.dynamic_slice_in_dim(
        jnp.concatenate([my_pairs, my_pairs]), lax.axis_index("core") * half, 2 * half, 0
    )
    text_ids = of_group(ids, TEXT_GROUP)
    logits = (
        similarity_multiplier
        * lax.dot_general(
            img_block, txt_block, (((1,), (1,)), ((), ())), preferred_element_type=jnp.float32
        )
        + shift
    )
    positive = (my_pairs[:, None] == text_ids[None, :]).astype(jnp.float32)
    sign = 2.0 * positive - 1.0
    loss = jnp.sum(jax.nn.softplus(-sign * logits), axis=1)
    slope = (jax.nn.sigmoid(logits) - positive).astype(jnp.bfloat16)
    txt_part = lax.dot_general(
        slope, img_block, (((0,), (0,)), ((), ())), preferred_element_type=jnp.float32
    )
    txt_terms = scatter((SEND_SCALE * txt_part).astype(jnp.float16), TEXT_GROUP)
    img_part = SEND_SCALE * jnp.dot(slope, txt_block, preferred_element_type=jnp.float32)
    img_part = jnp.concatenate(
        [img_part, jnp.broadcast_to(loss[:, None] * LOSS_SCALE, (2 * half, 128))], axis=1
    )
    came = lax.ppermute(img_part[half:].astype(jnp.float16), "core", [(0, 1), (1, 0)])
    img_sum = img_part[:half] + came.astype(jnp.float32)
    img_sum = img_sum.reshape(2, 2, 2, 2, own_rows, width + 128)
    img_sum = halve(img_sum, "z0", 2)
    img_sum = halve(img_sum, "z1", 1)
    img_sum = halve(img_sum, "z2", 0)
    img_sum = halve(img_sum, "y2", 0, txt_terms[0, 0, 0])
    loss = img_sum[:, width] / LOSS_SCALE
    img_sum = img_sum[:, :width]
    img_dir = (similarity_multiplier / SEND_SCALE) * img_sum
    txt_dir = (similarity_multiplier / SEND_SCALE) * jnp.sum(txt_terms.astype(jnp.float32), axis=0)
    unused, image_back = jax.vjp(normalize, picture_vectors.astype(jnp.float32))
    unused2, text_backward = jax.vjp(normalize, caption_vectors.astype(jnp.float32))
    return (image_back(img_dir)[0], text_backward(txt_dir)[0], loss)


def solution(mesh):
    fine = Mesh(mesh.devices.reshape(FINE_SIZES), FINE)
    in_specs = (P(FINE, None), P(FINE, None), P(), P(), P())
    out_specs = (P(FINE, None), P(FINE, None), P(FINE))
    return jax.shard_map(
        per_device, mesh=fine, in_specs=in_specs, out_specs=out_specs, check_vma=False
    )
```

```python
import jax
import jax.numpy as jnp
from jax import lax
from jax.sharding import Mesh, PartitionSpec as P

FINE = ("y2", "y1", "x", "core", "z", "y0")
FINE_SIZES = (2, 2, 8, 2, 8, 2)
IMAGE_GROUP = ("core", "z", "y2")
TEXT_GROUP = ("y1", "x", "y0")
SEND_SCALE = 2.0
LOSS_SCALE = 0.125


def normalize(raw):
    values = raw.astype(jnp.float32)
    return values * lax.rsqrt(jnp.sum(values * values, axis=1, keepdims=True) + 1e-06)


def shift_by(block, axis, step):
    count = lax.axis_size(axis)
    return lax.ppermute(block, axis, [(i, (i + step) % count) for i in range(count)])


def from_own(array, axis):
    return lax.dynamic_slice_in_dim(
        jnp.concatenate([array, array]), lax.axis_index(axis), array.shape[0], 0
    )


def gather(block, axes):
    copies = jnp.broadcast_to(block[None], (lax.axis_size(axes),) + block.shape)
    return lax.all_to_all(copies, axes, 0, 0, tiled=True)


def scatter(parts, axes):
    count = lax.axis_size(axes)
    return lax.all_to_all(
        parts.reshape(count, parts.shape[0] // count, parts.shape[1]), axes, 0, 0, tiled=True
    )


def half(total):
    return total.astype(jnp.float16)


def full(total):
    return total.astype(jnp.float32)


def per_device(
    picture_vectors,
    caption_vectors,
    caption_partner_position,
    sharpness_factor,
    affine_offset_array,
):
    own_rows, width = picture_vectors.shape
    similarity_multiplier = sharpness_factor[0]
    shift = affine_offset_array[0]
    own_images = normalize(picture_vectors).astype(jnp.bfloat16)
    txt_block = gather(normalize(caption_vectors).astype(jnp.bfloat16), TEXT_GROUP).reshape(-1, width)
    own_images = jnp.concatenate([own_images, shift_by(own_images, "y2", 1)])
    z_images = from_own(lax.all_gather(own_images, "z", axis=0, tiled=False), "z")
    z_images = z_images.reshape(-1, width)
    img_block = jnp.concatenate([z_images, shift_by(z_images, "core", 1)])
    image_count = img_block.shape[0]

    def of_group(array, group):
        rows = array.reshape(FINE_SIZES + (own_rows,))
        for place, axis in enumerate(FINE):
            if axis not in group:
                rows = lax.dynamic_slice_in_dim(rows, lax.axis_index(axis), 1, place)
        order = [FINE.index(axis) for axis in group]
        order = order + [i for i in range(len(FINE) + 1) if i not in order]
        return rows.transpose(order).reshape([lax.axis_size(axis) for axis in group] + [own_rows])

    ids = jnp.arange(caption_partner_position.shape[0], dtype=jnp.int32)
    text_ids = of_group(ids, TEXT_GROUP).reshape(-1)
    my_pairs = of_group(caption_partner_position, IMAGE_GROUP)
    for place, axis in enumerate(IMAGE_GROUP):
        my_pairs = jnp.moveaxis(from_own(jnp.moveaxis(my_pairs, place, 0), axis), 0, place)
    my_pairs = my_pairs.reshape(-1)
    logits = (
        similarity_multiplier
        * lax.dot_general(
            img_block, txt_block, (((1,), (1,)), ((), ())), preferred_element_type=jnp.float32
        )
        + shift
    )
    positive = (my_pairs[:, None] == text_ids[None, :]).astype(jnp.float32)
    sign = 2.0 * positive - 1.0
    loss = jnp.sum(jax.nn.softplus(-sign * logits), axis=1)
    slope = (jax.nn.sigmoid(logits) - positive).astype(jnp.bfloat16)
    txt_part = lax.dot_general(
        slope, img_block, (((0,), (0,)), ((), ())), preferred_element_type=jnp.float32
    )
    txt_terms = scatter(half(SEND_SCALE * txt_part), TEXT_GROUP)
    img_part = SEND_SCALE * jnp.dot(slope, txt_block, preferred_element_type=jnp.float32)
    img_part = jnp.concatenate(
        [img_part, jnp.broadcast_to(loss[:, None] * LOSS_SCALE, (image_count, 128))], axis=1
    ).reshape(2, 8, 2 * own_rows, width + 128)
    total = img_part[0] + full(shift_by(half(img_part[1]), "core", 1))
    far = shift_by(half(total[4]), "z", 4)
    ahead = full(shift_by(half(jnp.stack([total[1], total[3]])), "z", 1))
    back = full(shift_by(half(jnp.stack([total[7], total[5]])), "z", -1))
    near = total[0] + ahead[0] + back[0]
    near = near + full(shift_by(half(total[2] + ahead[1]), "z", 2))
    near = near + full(shift_by(half(total[6] + back[1]), "z", -2))
    near = near + full(far)
    tie = jnp.minimum(jnp.abs(txt_terms[0, 0, 0]), 0)
    total = near[:own_rows] + full(shift_by(half(near[own_rows:]) + tie, "y2", 1))
    loss = total[:, width] / LOSS_SCALE
    img_dir = (similarity_multiplier / SEND_SCALE) * total[:, :width]
    txt_dir = (similarity_multiplier / SEND_SCALE) * jnp.sum(full(txt_terms), axis=0)
    unused, image_back = jax.vjp(normalize, picture_vectors.astype(jnp.float32))
    unused2, text_backward = jax.vjp(normalize, caption_vectors.astype(jnp.float32))
    return (image_back(img_dir)[0], text_backward(txt_dir)[0], loss)


def solution(mesh):
    fine = Mesh(mesh.devices.reshape(FINE_SIZES), FINE)
    in_specs = (P(FINE, None), P(FINE, None), P(), P(), P())
    out_specs = (P(FINE, None), P(FINE, None), P(FINE))
    return jax.shard_map(
        per_device, mesh=fine, in_specs=in_specs, out_specs=out_specs, check_vma=False
    )
```

```python
import jax
import jax.numpy as jnp
from jax import lax
from jax.sharding import Mesh, PartitionSpec as P

FINE = ("yhi", "x", "core", "z", "ylo")
FINE_SIZES = (4, 8, 2, 8, 2)
IMAGE_GROUP = ("core", "z", "ylo")
TEXT_GROUP = ("yhi", "x")
SEND_SCALE = 2.0
LOSS_SCALE = 0.125


def normalize(raw):
    values = raw.astype(jnp.float32)
    return values * lax.rsqrt(jnp.sum(values * values, axis=1, keepdims=True) + 1e-06)


def shift_by(block, axis, step):
    count = lax.axis_size(axis)
    return lax.ppermute(block, axis, [(i, (i + step) % count) for i in range(count)])


def from_own(array, axis):
    return lax.dynamic_slice_in_dim(
        jnp.concatenate([array, array]), lax.axis_index(axis), array.shape[0], 0
    )


def gather(block, axes):
    copies = jnp.broadcast_to(block[None], (lax.axis_size(axes),) + block.shape)
    return lax.all_to_all(copies, axes, 0, 0, tiled=True)


def scatter(parts, axes):
    count = lax.axis_size(axes)
    return lax.all_to_all(
        parts.reshape(count, parts.shape[0] // count, parts.shape[1]), axes, 0, 0, tiled=True
    )


def half(total):
    return total.astype(jnp.float16)


def full(total):
    return total.astype(jnp.float32)


def per_device(
    picture_vectors,
    caption_vectors,
    caption_partner_position,
    sharpness_factor,
    affine_offset_array,
):
    own_rows, width = picture_vectors.shape
    similarity_multiplier = sharpness_factor[0]
    shift = affine_offset_array[0]
    own_images = normalize(picture_vectors).astype(jnp.bfloat16)
    neighbour_images = shift_by(own_images, "ylo", 1)
    own_images = jnp.concatenate([own_images, neighbour_images])
    own_texts = normalize(caption_vectors).astype(jnp.bfloat16)
    txt_block = gather(own_texts, TEXT_GROUP).reshape(-1, width)
    z_images = from_own(lax.all_gather(own_images, "z", axis=0, tiled=False), "z")
    z_images = z_images.reshape(-1, width)
    img_block = jnp.concatenate([z_images, shift_by(z_images, "core", 1)])
    image_count = img_block.shape[0]

    def of_group(array, group):
        rows = array.reshape(FINE_SIZES + (own_rows,))
        for place, axis in enumerate(FINE):
            if axis not in group:
                rows = lax.dynamic_slice_in_dim(rows, lax.axis_index(axis), 1, place)
        order = [FINE.index(axis) for axis in group]
        order = order + [i for i in range(len(FINE) + 1) if i not in order]
        return rows.transpose(order).reshape([lax.axis_size(axis) for axis in group] + [own_rows])

    ids = jnp.arange(caption_partner_position.shape[0], dtype=jnp.int32)
    text_ids = of_group(ids, TEXT_GROUP).reshape(-1)
    my_pairs = of_group(caption_partner_position, IMAGE_GROUP)
    for place, axis in enumerate(IMAGE_GROUP):
        my_pairs = jnp.moveaxis(from_own(jnp.moveaxis(my_pairs, place, 0), axis), 0, place)
    my_pairs = my_pairs.reshape(-1)
    logits = (
        similarity_multiplier
        * lax.dot_general(
            img_block, txt_block, (((1,), (1,)), ((), ())), preferred_element_type=jnp.float32
        )
        + shift
    )
    positive = (my_pairs[:, None] == text_ids[None, :]).astype(jnp.float32)
    sign = 2.0 * positive - 1.0
    loss = jnp.sum(jax.nn.softplus(-sign * logits), axis=1)
    slope = (jax.nn.sigmoid(logits) - positive).astype(jnp.bfloat16)
    txt_part = lax.dot_general(
        slope, img_block, (((0,), (0,)), ((), ())), preferred_element_type=jnp.float32
    )
    txt_terms = scatter(half(SEND_SCALE * txt_part), TEXT_GROUP)
    img_part = SEND_SCALE * jnp.dot(slope, txt_block, preferred_element_type=jnp.float32)
    img_part = jnp.concatenate(
        [img_part, jnp.broadcast_to(loss[:, None] * LOSS_SCALE, (image_count, 128))], axis=1
    ).reshape(2, 8, 2 * own_rows, width + 128)
    total = img_part[0] + full(shift_by(half(img_part[1]), "core", 1))
    far = shift_by(half(total[4]), "z", 4)
    ahead = full(shift_by(half(jnp.stack([total[1], total[3]])), "z", 1))
    back = full(shift_by(half(jnp.stack([total[7], total[5]])), "z", -1))
    near = total[0] + ahead[0] + back[0]
    near = near + full(shift_by(half(total[2] + ahead[1]), "z", 2))
    near = near + full(shift_by(half(total[6] + back[1]), "z", -2))
    near = near + full(far)
    total = near[:own_rows] + full(shift_by(half(near[own_rows:]), "ylo", 1))
    loss = total[:, width] / LOSS_SCALE
    img_dir = (similarity_multiplier / SEND_SCALE) * total[:, :width]
    txt_dir = (similarity_multiplier / SEND_SCALE) * jnp.sum(full(txt_terms), axis=0)
    unused, image_back = jax.vjp(normalize, picture_vectors.astype(jnp.float32))
    unused2, text_backward = jax.vjp(normalize, caption_vectors.astype(jnp.float32))
    return (image_back(img_dir)[0], text_backward(txt_dir)[0], loss)


def solution(mesh):
    fine = Mesh(mesh.devices.reshape(FINE_SIZES), FINE)
    in_specs = (P(FINE, None), P(FINE, None), P(), P(), P())
    out_specs = (P(FINE, None), P(FINE, None), P(FINE))
    return jax.shard_map(
        per_device, mesh=fine, in_specs=in_specs, out_specs=out_specs, check_vma=False
    )
```

```python
import jax
import jax.numpy as jnp
from jax import lax
from jax.sharding import Mesh, PartitionSpec as P

FINE = ("yhi", "x", "core", "z", "ylo")
FINE_SIZES = (4, 8, 2, 8, 2)
IMAGE_GROUP = ("core", "z", "ylo")
TEXT_GROUP = ("yhi", "x")
SEND_SCALE = 2.0
LOSS_SCALE = 0.125


def normalize(raw):
    values = raw.astype(jnp.float32)
    return values * lax.rsqrt(jnp.sum(values * values, axis=1, keepdims=True) + 1e-06)


def shift_by(block, axis, step):
    count = lax.axis_size(axis)
    return lax.ppermute(block, axis, [(i, (i + step) % count) for i in range(count)])


def from_own(array, axis):
    return lax.dynamic_slice_in_dim(
        jnp.concatenate([array, array]), lax.axis_index(axis), array.shape[0], 0
    )


def gather(block, axes):
    copies = jnp.broadcast_to(block[None], (lax.axis_size(axes),) + block.shape)
    return lax.all_to_all(copies, axes, 0, 0, tiled=True)


def scatter(parts, axes):
    count = lax.axis_size(axes)
    return lax.all_to_all(
        parts.reshape(count, parts.shape[0] // count, parts.shape[1]), axes, 0, 0, tiled=True
    )


def half(total):
    return total.astype(jnp.float16)


def full(total):
    return total.astype(jnp.float32)


def per_device(
    picture_vectors,
    caption_vectors,
    caption_partner_position,
    sharpness_factor,
    affine_offset_array,
):
    own_rows, width = picture_vectors.shape
    similarity_multiplier = sharpness_factor[0]
    shift = affine_offset_array[0]
    near_images = jnp.concatenate([picture_vectors, shift_by(picture_vectors, "ylo", 1)])
    own_images = normalize(near_images).astype(jnp.bfloat16)
    tie = jnp.minimum(jnp.abs(near_images[own_rows, 0]), 0)
    own_texts = normalize(caption_vectors).astype(jnp.bfloat16) + tie
    txt_block = gather(own_texts, TEXT_GROUP).reshape(-1, width)
    z_images = from_own(lax.all_gather(own_images, "z", axis=0, tiled=False), "z")
    z_images = z_images.reshape(-1, width)
    img_block = jnp.concatenate([z_images, shift_by(z_images, "core", 1)])
    image_count = img_block.shape[0]

    def of_group(array, group):
        rows = array.reshape(FINE_SIZES + (own_rows,))
        for place, axis in enumerate(FINE):
            if axis not in group:
                rows = lax.dynamic_slice_in_dim(rows, lax.axis_index(axis), 1, place)
        order = [FINE.index(axis) for axis in group]
        order = order + [i for i in range(len(FINE) + 1) if i not in order]
        return rows.transpose(order).reshape([lax.axis_size(axis) for axis in group] + [own_rows])

    ids = jnp.arange(caption_partner_position.shape[0], dtype=jnp.int32)
    text_ids = of_group(ids, TEXT_GROUP).reshape(-1)
    my_pairs = of_group(caption_partner_position, IMAGE_GROUP)
    for place, axis in enumerate(IMAGE_GROUP):
        my_pairs = jnp.moveaxis(from_own(jnp.moveaxis(my_pairs, place, 0), axis), 0, place)
    my_pairs = my_pairs.reshape(-1)
    logits = (
        similarity_multiplier
        * lax.dot_general(
            img_block, txt_block, (((1,), (1,)), ((), ())), preferred_element_type=jnp.float32
        )
        + shift
    )
    positive = (my_pairs[:, None] == text_ids[None, :]).astype(jnp.float32)
    sign = 2.0 * positive - 1.0
    loss = jnp.sum(jax.nn.softplus(-sign * logits), axis=1)
    slope = (jax.nn.sigmoid(logits) - positive).astype(jnp.bfloat16)
    txt_part = lax.dot_general(
        slope, img_block, (((0,), (0,)), ((), ())), preferred_element_type=jnp.float32
    )
    txt_terms = scatter(half(SEND_SCALE * txt_part), TEXT_GROUP)
    img_part = SEND_SCALE * jnp.dot(slope, txt_block, preferred_element_type=jnp.float32)
    img_part = jnp.concatenate(
        [img_part, jnp.broadcast_to(loss[:, None] * LOSS_SCALE, (image_count, 128))], axis=1
    ).reshape(2, 8, 2 * own_rows, width + 128)
    total = img_part[0] + full(shift_by(half(img_part[1]), "core", 1))
    far = shift_by(half(total[4]), "z", 4)
    ahead = full(shift_by(half(jnp.stack([total[1], total[3]])), "z", 1))
    back = full(shift_by(half(jnp.stack([total[7], total[5]])), "z", -1))
    near = total[0] + ahead[0] + back[0]
    near = near + full(shift_by(half(total[2] + ahead[1]), "z", 2))
    near = near + full(shift_by(half(total[6] + back[1]), "z", -2))
    near = near + full(far)
    total = near[:own_rows] + full(shift_by(half(near[own_rows:]), "ylo", 1))
    loss = total[:, width] / LOSS_SCALE
    img_dir = (similarity_multiplier / SEND_SCALE) * total[:, :width]
    txt_dir = (similarity_multiplier / SEND_SCALE) * jnp.sum(full(txt_terms), axis=0)
    unused, image_back = jax.vjp(normalize, picture_vectors.astype(jnp.float32))
    unused2, text_backward = jax.vjp(normalize, caption_vectors.astype(jnp.float32))
    return (image_back(img_dir)[0], text_backward(txt_dir)[0], loss)


def solution(mesh):
    fine = Mesh(mesh.devices.reshape(FINE_SIZES), FINE)
    in_specs = (P(FINE, None), P(FINE, None), P(), P(), P())
    out_specs = (P(FINE, None), P(FINE, None), P(FINE))
    return jax.shard_map(
        per_device, mesh=fine, in_specs=in_specs, out_specs=out_specs, check_vma=False
    )
```

```python
import jax
import jax.numpy as jnp
from jax import lax
from jax.experimental import pallas as pl
from jax.experimental.pallas import tpu as pltpu
from jax.sharding import Mesh, PartitionSpec as P

FINE = ("yhi", "xhi", "xlo", "core", "z", "ylo")
FINE_SIZES = (4, 4, 2, 2, 8, 2)
X = ("xhi", "xlo")
IMAGE_GROUP = ("core", "z", "ylo")
TEXT_GROUP = ("xlo", "yhi", "xhi")
SEND_SCALE = 2.0
LOSS_SCALE = 0.125


def normalize(raw):
    values = raw.astype(jnp.float32)
    return values * lax.rsqrt(jnp.sum(values * values, axis=1, keepdims=True) + 1e-06)


def shift_by(block, axis, step):
    count = lax.axis_size(axis)
    return lax.ppermute(block, axis, [(i, (i + step) % count) for i in range(count)])


def from_own(array, axis):
    return lax.dynamic_slice_in_dim(
        jnp.concatenate([array, array]), lax.axis_index(axis), array.shape[0], 0
    )


def copies_kernel(rows_ref, after_ref, copies_ref):
    for place in range(copies_ref.shape[0]):
        copies_ref[place] = rows_ref[...]


def gather(block, axes, after):
    count = lax.axis_size(axes)
    copies = pl.pallas_call(
        copies_kernel,
        out_shape=jax.ShapeDtypeStruct((count,) + block.shape, block.dtype),
        in_specs=[pl.BlockSpec(memory_space=pltpu.VMEM), pl.BlockSpec(memory_space=pl.ANY)],
        out_specs=pl.BlockSpec(memory_space=pltpu.VMEM),
        name="copies",
    )(block, after)
    return lax.all_to_all(copies, axes, 0, 0, tiled=True)


def scatter(parts, axes):
    count = lax.axis_size(axes)
    return lax.all_to_all(
        parts.reshape(count, parts.shape[0] // count, parts.shape[1]), axes, 0, 0, tiled=True
    )


def half(total):
    return total.astype(jnp.float16)


def full(total):
    return total.astype(jnp.float32)


def per_device(
    picture_vectors,
    caption_vectors,
    caption_partner_position,
    sharpness_factor,
    affine_offset_array,
):
    own_rows, width = picture_vectors.shape
    similarity_multiplier = sharpness_factor[0]
    shift = affine_offset_array[0]
    near_images = jnp.concatenate([picture_vectors, shift_by(picture_vectors, "ylo", 1)])
    own_images = normalize(near_images).astype(jnp.bfloat16)
    own_texts = normalize(caption_vectors).astype(jnp.bfloat16)
    near_texts = gather(own_texts, ("yhi", "xhi"), near_images[own_rows:]).reshape(-1, width)
    split = near_texts.shape[0] // 2
    xlo = lax.axis_index("xlo")
    txt_block = jnp.zeros((4 * split, width), jnp.bfloat16)
    for rows, place in (
        (near_texts, 2 * split * xlo),
        (shift_by(near_texts[:split], X, -1), 2 * split * (1 - xlo)),
        (shift_by(near_texts[split:], X, 1), 2 * split * (1 - xlo) + split),
    ):
        txt_block = lax.dynamic_update_slice_in_dim(txt_block, rows, place, 0)
    z_images = from_own(lax.all_gather(own_images, "z", axis=0, tiled=False), "z")
    z_images = z_images.reshape(-1, width)
    img_block = jnp.concatenate([z_images, shift_by(z_images, "core", 1)])
    image_count = img_block.shape[0]

    def of_group(array, group):
        rows = array.reshape(FINE_SIZES + (own_rows,))
        for place, axis in enumerate(FINE):
            if axis not in group:
                rows = lax.dynamic_slice_in_dim(rows, lax.axis_index(axis), 1, place)
        order = [FINE.index(axis) for axis in group]
        order = order + [i for i in range(len(FINE) + 1) if i not in order]
        return rows.transpose(order).reshape([lax.axis_size(axis) for axis in group] + [own_rows])

    ids = jnp.arange(caption_partner_position.shape[0], dtype=jnp.int32)
    text_ids = of_group(ids, TEXT_GROUP).reshape(-1)
    my_pairs = of_group(caption_partner_position, IMAGE_GROUP)
    for place, axis in enumerate(IMAGE_GROUP):
        my_pairs = jnp.moveaxis(from_own(jnp.moveaxis(my_pairs, place, 0), axis), 0, place)
    my_pairs = my_pairs.reshape(-1)
    logits = (
        similarity_multiplier
        * lax.dot_general(
            img_block, txt_block, (((1,), (1,)), ((), ())), preferred_element_type=jnp.float32
        )
        + shift
    )
    positive = (my_pairs[:, None] == text_ids[None, :]).astype(jnp.float32)
    sign = 2.0 * positive - 1.0
    loss = jnp.sum(jax.nn.softplus(-sign * logits), axis=1)
    slope = (jax.nn.sigmoid(logits) - positive).astype(jnp.bfloat16)
    txt_part = lax.dot_general(
        slope, img_block, (((0,), (0,)), ((), ())), preferred_element_type=jnp.float32
    )
    txt_terms = scatter(half(SEND_SCALE * txt_part), TEXT_GROUP)
    img_part = SEND_SCALE * jnp.dot(slope, txt_block, preferred_element_type=jnp.float32)
    img_part = jnp.concatenate(
        [img_part, jnp.broadcast_to(loss[:, None] * LOSS_SCALE, (image_count, 128))], axis=1
    ).reshape(2, 8, 2 * own_rows, width + 128)
    total = img_part[0] + full(shift_by(half(img_part[1]), "core", 1))
    far = shift_by(half(total[4]), "z", 4)
    ahead = full(shift_by(half(jnp.stack([total[1], total[3]])), "z", 1))
    back = full(shift_by(half(jnp.stack([total[7], total[5]])), "z", -1))
    near = total[0] + ahead[0] + back[0]
    near = near + full(shift_by(half(total[2] + ahead[1]), "z", 2))
    near = near + full(shift_by(half(total[6] + back[1]), "z", -2))
    near = near + full(far)
    total = near[:own_rows] + full(shift_by(half(near[own_rows:]), "ylo", 1))
    loss = total[:, width] / LOSS_SCALE
    img_dir = (similarity_multiplier / SEND_SCALE) * total[:, :width]
    txt_dir = (similarity_multiplier / SEND_SCALE) * jnp.sum(full(txt_terms), axis=0)
    unused, image_back = jax.vjp(normalize, picture_vectors.astype(jnp.float32))
    unused2, text_backward = jax.vjp(normalize, caption_vectors.astype(jnp.float32))
    return (image_back(img_dir)[0], text_backward(txt_dir)[0], loss)


def solution(mesh):
    fine = Mesh(mesh.devices.reshape(FINE_SIZES), FINE)
    in_specs = (P(FINE, None), P(FINE, None), P(), P(), P())
    out_specs = (P(FINE, None), P(FINE, None), P(FINE))
    return jax.shard_map(
        per_device, mesh=fine, in_specs=in_specs, out_specs=out_specs, check_vma=False
    )
```

```python
import jax
import jax.numpy as jnp
from jax import lax
from jax.experimental import pallas as pl
from jax.experimental.pallas import tpu as pltpu
from jax.sharding import Mesh, PartitionSpec as P

FINE = ("yhi", "x", "core", "z", "ylo")
FINE_SIZES = (4, 8, 2, 8, 2)
IMAGE_GROUP = ("core", "z", "ylo")
TEXT_GROUP = ("yhi", "x")
SEND_SCALE = 2.0
LOSS_SCALE = 0.125
WAIT_FLOPS = 100_000_000_000


def normalize(raw):
    values = raw.astype(jnp.float32)
    return values * lax.rsqrt(jnp.sum(values * values, axis=1, keepdims=True) + 1e-06)


def shift_by(block, axis, step):
    count = lax.axis_size(axis)
    return lax.ppermute(block, axis, [(i, (i + step) % count) for i in range(count)])


def from_own(array, axis):
    return lax.dynamic_slice_in_dim(
        jnp.concatenate([array, array]), lax.axis_index(axis), array.shape[0], 0
    )


def copies_kernel(raw_ref, copies_ref):
    rows = normalize(raw_ref[...]).astype(copies_ref.dtype)
    for place in range(copies_ref.shape[0]):
        copies_ref[place] = rows


def gather(raw, axes):
    copies = pl.pallas_call(
        copies_kernel,
        out_shape=jax.ShapeDtypeStruct((lax.axis_size(axes),) + raw.shape, jnp.bfloat16),
        in_specs=[pl.BlockSpec(memory_space=pltpu.VMEM)],
        out_specs=pl.BlockSpec(memory_space=pltpu.VMEM),
        name="copies",
    )(raw)
    return lax.all_to_all(copies, axes, 0, 0, tiled=True)


def rows_kernel(first_ref, second_ref, rows_ref):
    count = first_ref.shape[0]
    rows_ref[:count] = normalize(first_ref[...]).astype(rows_ref.dtype)
    rows_ref[count:] = normalize(second_ref[...]).astype(rows_ref.dtype)


def normalized_rows(first, second):
    return pl.pallas_call(
        rows_kernel,
        out_shape=jax.ShapeDtypeStruct((2 * first.shape[0], first.shape[1]), jnp.bfloat16),
        in_specs=[pl.BlockSpec(memory_space=pltpu.VMEM)] * 2,
        out_specs=pl.BlockSpec(memory_space=pltpu.VMEM),
        cost_estimate=pl.CostEstimate(flops=WAIT_FLOPS, bytes_accessed=0, transcendentals=0),
        name="rows",
    )(first, second)


def scatter(parts, axes):
    count = lax.axis_size(axes)
    return lax.all_to_all(
        parts.reshape(count, parts.shape[0] // count, parts.shape[1]), axes, 0, 0, tiled=True
    )


def half(total):
    return total.astype(jnp.float16)


def full(total):
    return total.astype(jnp.float32)


def per_device(
    picture_vectors,
    caption_vectors,
    caption_partner_position,
    sharpness_factor,
    affine_offset_array,
):
    own_rows, width = picture_vectors.shape
    similarity_multiplier = sharpness_factor[0]
    shift = affine_offset_array[0]
    own_images = normalized_rows(picture_vectors, shift_by(picture_vectors, "ylo", 1))
    txt_block = gather(caption_vectors, TEXT_GROUP).reshape(-1, width)
    z_images = from_own(lax.all_gather(own_images, "z", axis=0, tiled=False), "z")
    z_images = z_images.reshape(-1, width)
    img_block = jnp.concatenate([z_images, shift_by(z_images, "core", 1)])
    image_count = img_block.shape[0]

    def of_group(array, group):
        rows = array.reshape(FINE_SIZES + (own_rows,))
        for place, axis in enumerate(FINE):
            if axis not in group:
                rows = lax.dynamic_slice_in_dim(rows, lax.axis_index(axis), 1, place)
        order = [FINE.index(axis) for axis in group]
        order = order + [i for i in range(len(FINE) + 1) if i not in order]
        return rows.transpose(order).reshape([lax.axis_size(axis) for axis in group] + [own_rows])

    ids = jnp.arange(caption_partner_position.shape[0], dtype=jnp.int32)
    text_ids = of_group(ids, TEXT_GROUP).reshape(-1)
    my_pairs = of_group(caption_partner_position, IMAGE_GROUP)
    for place, axis in enumerate(IMAGE_GROUP):
        my_pairs = jnp.moveaxis(from_own(jnp.moveaxis(my_pairs, place, 0), axis), 0, place)
    my_pairs = my_pairs.reshape(-1)
    logits = (
        similarity_multiplier
        * lax.dot_general(
            img_block, txt_block, (((1,), (1,)), ((), ())), preferred_element_type=jnp.float32
        )
        + shift
    )
    positive = (my_pairs[:, None] == text_ids[None, :]).astype(jnp.float32)
    sign = 2.0 * positive - 1.0
    loss = jnp.sum(jax.nn.softplus(-sign * logits), axis=1)
    slope = (jax.nn.sigmoid(logits) - positive).astype(jnp.bfloat16)
    txt_part = lax.dot_general(
        slope, img_block, (((0,), (0,)), ((), ())), preferred_element_type=jnp.float32
    )
    txt_terms = scatter(half(SEND_SCALE * txt_part), TEXT_GROUP)
    img_part = SEND_SCALE * jnp.dot(slope, txt_block, preferred_element_type=jnp.float32)
    img_part = jnp.concatenate(
        [img_part, jnp.broadcast_to(loss[:, None] * LOSS_SCALE, (image_count, 128))], axis=1
    ).reshape(2, 8, 2 * own_rows, width + 128)
    total = img_part[0] + shift_by(img_part[1], "core", 1)
    far = shift_by(half(total[4]), "z", 4)
    ahead = full(shift_by(half(jnp.stack([total[1], total[3]])), "z", 1))
    back = full(shift_by(half(jnp.stack([total[7], total[5]])), "z", -1))
    near = total[0] + ahead[0] + back[0]
    near = near + full(shift_by(half(total[2] + ahead[1]), "z", 2))
    near = near + full(shift_by(half(total[6] + back[1]), "z", -2))
    near = near + full(far)
    total = near[:own_rows] + full(shift_by(half(near[own_rows:]), "ylo", 1))
    loss = total[:, width] / LOSS_SCALE
    img_dir = (similarity_multiplier / SEND_SCALE) * total[:, :width]
    txt_dir = (similarity_multiplier / SEND_SCALE) * jnp.sum(full(txt_terms), axis=0)
    unused, image_back = jax.vjp(normalize, picture_vectors.astype(jnp.float32))
    unused2, text_backward = jax.vjp(normalize, caption_vectors.astype(jnp.float32))
    return (image_back(img_dir)[0], text_backward(txt_dir)[0], loss)


def solution(mesh):
    fine = Mesh(mesh.devices.reshape(FINE_SIZES), FINE)
    in_specs = (P(FINE, None), P(FINE, None), P(), P(), P())
    out_specs = (P(FINE, None), P(FINE, None), P(FINE))
    return jax.shard_map(
        per_device, mesh=fine, in_specs=in_specs, out_specs=out_specs, check_vma=False
    )
```

```python
import jax
import jax.numpy as jnp
from jax import lax
from jax.experimental import pallas as pl
from jax.experimental.pallas import tpu as pltpu
from jax.sharding import Mesh, PartitionSpec as P

FINE = ("yhi", "x", "core", "z", "ylo")
FINE_SIZES = (4, 8, 2, 8, 2)
IMAGE_GROUP = ("core", "z", "ylo")
TEXT_GROUP = ("yhi", "x")
SEND_SCALE = 2.0
LOSS_SCALE = 0.125
WAIT_FLOPS = 100_000_000_000


def normalize(raw):
    values = raw.astype(jnp.float32)
    return values * lax.rsqrt(jnp.sum(values * values, axis=1, keepdims=True) + 1e-06)


def shift_by(block, axis, step):
    count = lax.axis_size(axis)
    return lax.ppermute(block, axis, [(i, (i + step) % count) for i in range(count)])


def from_own(array, axis):
    return lax.dynamic_slice_in_dim(
        jnp.concatenate([array, array]), lax.axis_index(axis), array.shape[0], 0
    )


def copies_kernel(raw_ref, copies_ref):
    rows = normalize(raw_ref[...]).astype(copies_ref.dtype)
    for place in range(copies_ref.shape[0]):
        copies_ref[place] = rows


def gather(raw, axes):
    copies = pl.pallas_call(
        copies_kernel,
        out_shape=jax.ShapeDtypeStruct((lax.axis_size(axes),) + raw.shape, jnp.bfloat16),
        in_specs=[pl.BlockSpec(memory_space=pltpu.VMEM)],
        out_specs=pl.BlockSpec(memory_space=pltpu.VMEM),
        name="copies",
    )(raw)
    return lax.all_to_all(copies, axes, 0, 0, tiled=True)


def pairs_kernel(place_ref, all_ref, pairs_ref):
    group, core, z, ylo = place_ref[0], place_ref[1], place_ref[2], place_ref[3]
    lane = lax.broadcasted_iota(jnp.int32, (1, 128), 1)
    turn = lax.rem(z, 4) * 32
    for ahead in range(2):
        first = group * 4 + lax.rem(core + ahead, 2) * 2
        rows = []
        for late in range(2):
            row = all_ref[pl.ds(first + lax.rem(z // 4 + late, 2), 1), :]
            swapped = jnp.where(lane % 32 < 16, pltpu.roll(row, 112, 1), pltpu.roll(row, 16, 1))
            rows.append(pltpu.roll(jnp.where(ylo == 0, row, swapped), lax.rem(128 - turn, 128), 1))
        pairs_ref[2 * ahead : 2 * ahead + 1, :] = jnp.where(lane + turn < 128, rows[0], rows[1])
        pairs_ref[2 * ahead + 1 : 2 * ahead + 2, :] = jnp.where(lane + turn < 128, rows[1], rows[0])


def image_pairs(caption_partner_position, image_count):
    place = jnp.stack([lax.axis_index(axes) for axes in (TEXT_GROUP,) + IMAGE_GROUP]).astype(jnp.int32)
    pairs = pl.pallas_call(
        pairs_kernel,
        out_shape=jax.ShapeDtypeStruct((image_count // 128, 128), jnp.int32),
        in_specs=[
            pl.BlockSpec(memory_space=pltpu.SMEM),
            pl.BlockSpec(memory_space=pltpu.VMEM),
        ],
        out_specs=pl.BlockSpec(memory_space=pltpu.VMEM),
        cost_estimate=pl.CostEstimate(flops=WAIT_FLOPS, bytes_accessed=0, transcendentals=0),
        name="pairs",
    )(place, caption_partner_position.reshape(-1, 128))
    return pairs.reshape(-1)


def scatter(parts, axes):
    count = lax.axis_size(axes)
    return lax.all_to_all(
        parts.reshape(count, parts.shape[0] // count, parts.shape[1]), axes, 0, 0, tiled=True
    )


def half(total):
    return total.astype(jnp.float16)


def full(total):
    return total.astype(jnp.float32)


def per_device(
    picture_vectors,
    caption_vectors,
    caption_partner_position,
    sharpness_factor,
    affine_offset_array,
):
    own_rows, width = picture_vectors.shape
    similarity_multiplier = sharpness_factor[0]
    shift = affine_offset_array[0]
    raw_images = jnp.concatenate([picture_vectors, shift_by(picture_vectors, "ylo", 1)])
    txt_block = gather(caption_vectors, TEXT_GROUP).reshape(-1, width)
    raw_images = lax.all_gather(raw_images, "z", axis=0, tiled=False)
    z_images = normalize(from_own(raw_images, "z").reshape(-1, width)).astype(jnp.bfloat16)
    img_block = jnp.concatenate([z_images, shift_by(z_images, "core", 1)])
    image_count = img_block.shape[0]
    my_pairs = image_pairs(caption_partner_position, image_count)
    column = jnp.arange(txt_block.shape[0], dtype=jnp.int32)
    text_ids = (
        column // own_rows * image_count + lax.axis_index(IMAGE_GROUP) * own_rows + column % own_rows
    )
    logits = (
        similarity_multiplier
        * lax.dot_general(
            img_block, txt_block, (((1,), (1,)), ((), ())), preferred_element_type=jnp.float32
        )
        + shift
    )
    positive = (my_pairs[:, None] == text_ids[None, :]).astype(jnp.float32)
    sign = 2.0 * positive - 1.0
    loss = jnp.sum(jax.nn.softplus(-sign * logits), axis=1)
    slope = (jax.nn.sigmoid(logits) - positive).astype(jnp.bfloat16)
    txt_part = lax.dot_general(
        slope, img_block, (((0,), (0,)), ((), ())), preferred_element_type=jnp.float32
    )
    txt_terms = scatter(half(SEND_SCALE * txt_part), TEXT_GROUP)
    img_part = SEND_SCALE * jnp.dot(slope, txt_block, preferred_element_type=jnp.float32)
    img_part = jnp.concatenate(
        [img_part, jnp.broadcast_to(loss[:, None] * LOSS_SCALE, (image_count, 128))], axis=1
    ).reshape(2, 8, 2 * own_rows, width + 128)
    total = img_part[0] + full(shift_by(half(img_part[1]), "core", 1))
    far = shift_by(half(total[4]), "z", 4)
    ahead = full(shift_by(half(jnp.stack([total[1], total[3]])), "z", 1))
    back = full(shift_by(half(jnp.stack([total[7], total[5]])), "z", -1))
    near = total[0] + ahead[0] + back[0]
    near = near + full(shift_by(half(total[2] + ahead[1]), "z", 2))
    near = near + full(shift_by(half(total[6] + back[1]), "z", -2))
    near = near + full(far)
    total = near[:own_rows] + full(shift_by(half(near[own_rows:]), "ylo", 1))
    loss = total[:, width] / LOSS_SCALE
    img_dir = (similarity_multiplier / SEND_SCALE) * total[:, :width]
    txt_dir = (similarity_multiplier / SEND_SCALE) * jnp.sum(full(txt_terms), axis=0)
    unused, image_back = jax.vjp(normalize, picture_vectors.astype(jnp.float32))
    unused2, text_backward = jax.vjp(normalize, caption_vectors.astype(jnp.float32))
    return (image_back(img_dir)[0], text_backward(txt_dir)[0], loss)


def solution(mesh):
    fine = Mesh(mesh.devices.reshape(FINE_SIZES), FINE)
    in_specs = (P(FINE, None), P(FINE, None), P(), P(), P())
    out_specs = (P(FINE, None), P(FINE, None), P(FINE))
    return jax.shard_map(
        per_device, mesh=fine, in_specs=in_specs, out_specs=out_specs, check_vma=False
    )
```

```python
import jax
import jax.numpy as jnp
from jax import lax
from jax.experimental import pallas as pl
from jax.experimental.pallas import tpu as pltpu
from jax.sharding import Mesh, PartitionSpec as P

FINE = ("yhi", "x", "core", "z", "ylo")
FINE_SIZES = (4, 8, 2, 8, 2)
IMAGE_GROUP = ("core", "z", "ylo")
Z_ORDER = (0, 2, 6, 4, 1, 3, 7, 5)
TEXT_GROUP = ("yhi", "x")
SEND_SCALE = 2.0
LOSS_SCALE = 0.125
WAIT_FLOPS = 100_000_000_000


def normalize(raw):
    values = raw.astype(jnp.float32)
    return values * lax.rsqrt(jnp.sum(values * values, axis=1, keepdims=True) + 1e-06)


def shift_by(block, axis, step):
    count = lax.axis_size(axis)
    return lax.ppermute(block, axis, [(i, (i + step) % count) for i in range(count)])


def gather_z(own):
    two_on, two_back = shift_by(own, "z", -2), shift_by(own, "z", 2)
    on = shift_by(jnp.concatenate([own, two_on]), "z", -1)
    back = shift_by(jnp.concatenate([own, two_back]), "z", 1)
    return jnp.concatenate([own, two_on, two_back, shift_by(own, "z", 4), on, back])


def copies_kernel(raw_ref, copies_ref):
    rows = normalize(raw_ref[...]).astype(copies_ref.dtype)
    for place in range(copies_ref.shape[0]):
        copies_ref[place] = rows


def gather(raw, axes):
    copies = pl.pallas_call(
        copies_kernel,
        out_shape=jax.ShapeDtypeStruct((lax.axis_size(axes),) + raw.shape, jnp.bfloat16),
        in_specs=[pl.BlockSpec(memory_space=pltpu.VMEM)],
        out_specs=pl.BlockSpec(memory_space=pltpu.VMEM),
        name="copies",
    )(raw)
    return lax.all_to_all(copies, axes, 0, 0, tiled=True)


def pairs_kernel(place_ref, all_ref, pairs_ref):
    group, core, z, ylo = place_ref[0], place_ref[1], place_ref[2], place_ref[3]
    lane = lax.broadcasted_iota(jnp.int32, (1, 128), 1)
    for ahead in range(2):
        first = group * 4 + lax.rem(core + ahead, 2) * 2
        for line in range(2):
            row = jnp.zeros((1, 128), jnp.int32)
            for slot, distance in enumerate(Z_ORDER[4 * line : 4 * line + 4]):
                there = lax.rem(z + distance, 8)
                held = all_ref[pl.ds(first + there // 4, 1), :]
                held = pltpu.roll(held, lax.rem(128 + 32 * slot - 32 * lax.rem(there, 4), 128), 1)
                row = jnp.where(lane // 32 == slot, held, row)
            swapped = jnp.where(lane % 32 < 16, pltpu.roll(row, 112, 1), pltpu.roll(row, 16, 1))
            out = 2 * ahead + line
            pairs_ref[out : out + 1, :] = jnp.where(ylo == 0, row, swapped)


def image_pairs(caption_partner_position, image_count):
    place = jnp.stack([lax.axis_index(axes) for axes in (TEXT_GROUP,) + IMAGE_GROUP]).astype(jnp.int32)
    pairs = pl.pallas_call(
        pairs_kernel,
        out_shape=jax.ShapeDtypeStruct((image_count // 128, 128), jnp.int32),
        in_specs=[
            pl.BlockSpec(memory_space=pltpu.SMEM),
            pl.BlockSpec(memory_space=pltpu.VMEM),
        ],
        out_specs=pl.BlockSpec(memory_space=pltpu.VMEM),
        cost_estimate=pl.CostEstimate(flops=WAIT_FLOPS, bytes_accessed=0, transcendentals=0),
        name="pairs",
    )(place, caption_partner_position.reshape(-1, 128))
    return pairs.reshape(-1)


def scatter(parts, axes):
    count = lax.axis_size(axes)
    return lax.all_to_all(
        parts.reshape(count, parts.shape[0] // count, parts.shape[1]), axes, 0, 0, tiled=True
    )


def half(total):
    return total.astype(jnp.float16)


def full(total):
    return total.astype(jnp.float32)


def per_device(
    picture_vectors,
    caption_vectors,
    caption_partner_position,
    sharpness_factor,
    affine_offset_array,
):
    own_rows, width = picture_vectors.shape
    similarity_multiplier = sharpness_factor[0]
    shift = affine_offset_array[0]
    near_images = jnp.concatenate([picture_vectors, shift_by(picture_vectors, "ylo", 1)])
    near_images = normalize(near_images).astype(jnp.bfloat16)
    txt_block = gather(caption_vectors, TEXT_GROUP).reshape(-1, width)
    z_images = gather_z(near_images)
    img_block = jnp.concatenate([z_images, shift_by(z_images, "core", 1)])
    image_count = img_block.shape[0]
    my_pairs = image_pairs(caption_partner_position, image_count)
    column = jnp.arange(txt_block.shape[0], dtype=jnp.int32)
    text_ids = (
        column // own_rows * image_count + lax.axis_index(IMAGE_GROUP) * own_rows + column % own_rows
    )
    logits = (
        similarity_multiplier
        * lax.dot_general(
            img_block, txt_block, (((1,), (1,)), ((), ())), preferred_element_type=jnp.float32
        )
        + shift
    )
    positive = (my_pairs[:, None] == text_ids[None, :]).astype(jnp.float32)
    sign = 2.0 * positive - 1.0
    loss = jnp.sum(jax.nn.softplus(-sign * logits), axis=1)
    slope = (jax.nn.sigmoid(logits) - positive).astype(jnp.bfloat16)
    txt_part = lax.dot_general(
        slope, img_block, (((0,), (0,)), ((), ())), preferred_element_type=jnp.float32
    )
    txt_terms = scatter(half(SEND_SCALE * txt_part), TEXT_GROUP)
    img_part = SEND_SCALE * jnp.dot(slope, txt_block, preferred_element_type=jnp.float32)
    img_part = jnp.concatenate(
        [img_part, jnp.broadcast_to(loss[:, None] * LOSS_SCALE, (image_count, 128))], axis=1
    ).reshape(2, 8, 2 * own_rows, width + 128)
    total = img_part[0] + full(shift_by(half(img_part[1]), "core", 1))
    far = shift_by(half(total[3]), "z", 4)
    ahead = full(shift_by(half(total[4:6]), "z", 1))
    back = full(shift_by(half(total[6:8]), "z", -1))
    near = total[0] + ahead[0] + back[0]
    near = near + full(shift_by(half(total[1] + ahead[1]), "z", 2))
    near = near + full(shift_by(half(total[2] + back[1]), "z", -2))
    near = near + full(far)
    total = near[:own_rows] + full(shift_by(half(near[own_rows:]), "ylo", 1))
    loss = total[:, width] / LOSS_SCALE
    img_dir = (similarity_multiplier / SEND_SCALE) * total[:, :width]
    txt_dir = (similarity_multiplier / SEND_SCALE) * jnp.sum(full(txt_terms), axis=0)
    unused, image_back = jax.vjp(normalize, picture_vectors.astype(jnp.float32))
    unused2, text_backward = jax.vjp(normalize, caption_vectors.astype(jnp.float32))
    return (image_back(img_dir)[0], text_backward(txt_dir)[0], loss)


def solution(mesh):
    fine = Mesh(mesh.devices.reshape(FINE_SIZES), FINE)
    in_specs = (P(FINE, None), P(FINE, None), P(), P(), P())
    out_specs = (P(FINE, None), P(FINE, None), P(FINE))
    return jax.shard_map(
        per_device, mesh=fine, in_specs=in_specs, out_specs=out_specs, check_vma=False
    )
```

```python
import jax
import jax.numpy as jnp
from jax import lax
from jax.experimental import pallas as pl
from jax.experimental.pallas import tpu as pltpu
from jax.sharding import Mesh, PartitionSpec as P

FINE = ("yhi", "x", "core", "z", "ylo")
FINE_SIZES = (4, 8, 2, 8, 2)
IMAGE_GROUP = ("core", "z", "ylo")
TEXT_GROUP = ("yhi", "x")
SEND_SCALE = 2.0
LOSS_SCALE = 0.125
WAIT_FLOPS = 100_000_000_000
KERNEL_BYTES = 4 * 1024 * 1024


def normalize(raw):
    values = raw.astype(jnp.float32)
    return values * lax.rsqrt(jnp.sum(values * values, axis=1, keepdims=True) + 1e-06)


def shift_by(block, axis, step):
    count = lax.axis_size(axis)
    return lax.ppermute(block, axis, [(i, (i + step) % count) for i in range(count)])


def from_own(array, axis):
    return lax.dynamic_slice_in_dim(
        jnp.concatenate([array, array]), lax.axis_index(axis), array.shape[0], 0
    )


def copies_kernel(raw_ref, copies_ref):
    rows = normalize(raw_ref[...]).astype(copies_ref.dtype)
    for place in range(copies_ref.shape[0]):
        copies_ref[place] = rows


def gather(raw, axes):
    copies = pl.pallas_call(
        copies_kernel,
        out_shape=jax.ShapeDtypeStruct((lax.axis_size(axes),) + raw.shape, jnp.bfloat16),
        in_specs=[pl.BlockSpec(memory_space=pltpu.VMEM)],
        out_specs=pl.BlockSpec(memory_space=pltpu.VMEM),
        compiler_params=pltpu.CompilerParams(vmem_limit_bytes=KERNEL_BYTES),
        name="copies",
    )(raw)
    return lax.all_to_all(copies, axes, 0, 0, tiled=True)


def pairs_kernel(all_ref, pairs_ref):
    group = lax.axis_index(TEXT_GROUP)
    core, z, ylo = [lax.axis_index(axis) for axis in IMAGE_GROUP]
    lane = lax.broadcasted_iota(jnp.int32, (1, 128), 1)
    turn = lax.rem(z, 4) * 32
    for ahead in range(2):
        first = group * 4 + lax.rem(core + ahead, 2) * 2
        rows = []
        for late in range(2):
            row = all_ref[pl.ds(first + lax.rem(z // 4 + late, 2), 1), :]
            swapped = jnp.where(lane % 32 < 16, pltpu.roll(row, 112, 1), pltpu.roll(row, 16, 1))
            rows.append(pltpu.roll(jnp.where(ylo == 0, row, swapped), lax.rem(128 - turn, 128), 1))
        pairs_ref[2 * ahead : 2 * ahead + 1, :] = jnp.where(lane + turn < 128, rows[0], rows[1])
        pairs_ref[2 * ahead + 1 : 2 * ahead + 2, :] = jnp.where(lane + turn < 128, rows[1], rows[0])


def image_pairs(caption_partner_position, image_count):
    pairs = pl.pallas_call(
        pairs_kernel,
        out_shape=jax.ShapeDtypeStruct((image_count // 128, 128), jnp.int32),
        in_specs=[pl.BlockSpec(memory_space=pltpu.VMEM)],
        out_specs=pl.BlockSpec(memory_space=pltpu.VMEM),
        cost_estimate=pl.CostEstimate(flops=WAIT_FLOPS, bytes_accessed=0, transcendentals=0),
        compiler_params=pltpu.CompilerParams(vmem_limit_bytes=KERNEL_BYTES),
        name="pairs",
    )(caption_partner_position.reshape(-1, 128))
    return pairs.reshape(-1)


def scatter(parts, axes):
    count = lax.axis_size(axes)
    return lax.all_to_all(
        parts.reshape(count, parts.shape[0] // count, parts.shape[1]), axes, 0, 0, tiled=True
    )


def half(total):
    return total.astype(jnp.float16)


def full(total):
    return total.astype(jnp.float32)


def per_device(
    picture_vectors,
    caption_vectors,
    caption_partner_position,
    sharpness_factor,
    affine_offset_array,
):
    own_rows, width = picture_vectors.shape
    similarity_multiplier = sharpness_factor[0]
    shift = affine_offset_array[0]
    near_images = jnp.concatenate([picture_vectors, shift_by(picture_vectors, "ylo", 1)])
    near_images = normalize(near_images).astype(jnp.bfloat16)
    txt_block = gather(caption_vectors, TEXT_GROUP).reshape(-1, width)
    z_images = from_own(lax.all_gather(near_images, "z", axis=0, tiled=False), "z").reshape(-1, width)
    img_block = jnp.concatenate([z_images, shift_by(z_images, "core", 1)])
    image_count = img_block.shape[0]
    my_pairs = image_pairs(caption_partner_position, image_count)
    column = jnp.arange(txt_block.shape[0], dtype=jnp.int32)
    text_ids = (
        column // own_rows * image_count + lax.axis_index(IMAGE_GROUP) * own_rows + column % own_rows
    )
    logits = (
        similarity_multiplier
        * lax.dot_general(
            img_block, txt_block, (((1,), (1,)), ((), ())), preferred_element_type=jnp.float32
        )
        + shift
    )
    positive = (my_pairs[:, None] == text_ids[None, :]).astype(jnp.float32)
    sign = 2.0 * positive - 1.0
    loss = jnp.sum(jax.nn.softplus(-sign * logits), axis=1)
    slope = (jax.nn.sigmoid(logits) - positive).astype(jnp.bfloat16)
    txt_part = lax.dot_general(
        slope, img_block, (((0,), (0,)), ((), ())), preferred_element_type=jnp.float32
    )
    txt_terms = scatter(half(SEND_SCALE * txt_part), TEXT_GROUP)
    img_part = SEND_SCALE * jnp.dot(slope, txt_block, preferred_element_type=jnp.float32)
    img_part = jnp.concatenate(
        [img_part, jnp.broadcast_to(loss[:, None] * LOSS_SCALE, (image_count, 128))], axis=1
    ).reshape(2, 8, 2 * own_rows, width + 128)
    total = img_part[0] + full(shift_by(half(img_part[1]), "core", 1))
    far = shift_by(half(total[4]), "z", 4)
    ahead = full(shift_by(half(jnp.stack([total[1], total[3]])), "z", 1))
    back = full(shift_by(half(jnp.stack([total[7], total[5]])), "z", -1))
    near = total[0] + ahead[0] + back[0]
    near = near + full(shift_by(half(total[2] + ahead[1]), "z", 2))
    near = near + full(shift_by(half(total[6] + back[1]), "z", -2))
    near = near + full(far)
    total = near[:own_rows] + full(shift_by(half(near[own_rows:]), "ylo", 1))
    loss = total[:, width] / LOSS_SCALE
    img_dir = (similarity_multiplier / SEND_SCALE) * total[:, :width]
    txt_dir = (similarity_multiplier / SEND_SCALE) * jnp.sum(full(txt_terms), axis=0)
    unused, image_back = jax.vjp(normalize, picture_vectors.astype(jnp.float32))
    unused2, text_backward = jax.vjp(normalize, caption_vectors.astype(jnp.float32))
    return (image_back(img_dir)[0], text_backward(txt_dir)[0], loss)


def solution(mesh):
    fine = Mesh(mesh.devices.reshape(FINE_SIZES), FINE)
    in_specs = (P(FINE, None), P(FINE, None), P(), P(), P())
    out_specs = (P(FINE, None), P(FINE, None), P(FINE))
    return jax.shard_map(
        per_device, mesh=fine, in_specs=in_specs, out_specs=out_specs, check_vma=False
    )
```

```python
import jax
import jax.numpy as jnp
from jax import lax
from jax.experimental import pallas as pl
from jax.experimental.pallas import tpu as pltpu
from jax.sharding import Mesh, PartitionSpec as P

FINE = ("yhi", "x", "core", "z", "ylo")
FINE_SIZES = (4, 8, 2, 8, 2)
IMAGE_GROUP = ("core", "z", "ylo")
TEXT_GROUP = ("yhi", "x")
SEND_SCALE = 2.0
LOSS_SCALE = 0.125
WAIT_FLOPS = 100_000_000_000
KERNEL_BYTES = 4 * 1024 * 1024


def normalize(raw):
    values = raw.astype(jnp.float32)
    return values * lax.rsqrt(jnp.sum(values * values, axis=1, keepdims=True) + 1e-06)


def shift_by(block, axis, step):
    count = lax.axis_size(axis)
    return lax.ppermute(block, axis, [(i, (i + step) % count) for i in range(count)])


def from_own(array, axis):
    return lax.dynamic_slice_in_dim(
        jnp.concatenate([array, array]), lax.axis_index(axis), array.shape[0], 0
    )


def copies_kernel(raw_ref, copies_ref):
    rows = normalize(raw_ref[...]).astype(copies_ref.dtype)
    for place in range(copies_ref.shape[0]):
        copies_ref[place] = rows


def gather(raw, axes):
    copies = pl.pallas_call(
        copies_kernel,
        out_shape=jax.ShapeDtypeStruct((lax.axis_size(axes),) + raw.shape, jnp.bfloat16),
        in_specs=[pl.BlockSpec(memory_space=pltpu.VMEM)],
        out_specs=pl.BlockSpec(memory_space=pltpu.VMEM),
        compiler_params=pltpu.CompilerParams(vmem_limit_bytes=KERNEL_BYTES),
        name="copies",
    )(raw)
    return lax.all_to_all(copies, axes, 0, 0, tiled=True)


def pairs_kernel(all_ref, pairs_ref):
    group = lax.axis_index(TEXT_GROUP)
    core, z, ylo = [lax.axis_index(axis) for axis in IMAGE_GROUP]
    lane = lax.broadcasted_iota(jnp.int32, (1, 128), 1)
    turn = lax.rem(z, 4) * 32
    for ahead in range(2):
        first = group * 4 + lax.rem(core + ahead, 2) * 2
        rows = []
        for late in range(2):
            row = all_ref[pl.ds(first + lax.rem(z // 4 + late, 2), 1), :]
            swapped = jnp.where(lane % 32 < 16, pltpu.roll(row, 112, 1), pltpu.roll(row, 16, 1))
            rows.append(pltpu.roll(jnp.where(ylo == 0, row, swapped), lax.rem(128 - turn, 128), 1))
        pairs_ref[2 * ahead : 2 * ahead + 1, :] = jnp.where(lane + turn < 128, rows[0], rows[1])
        pairs_ref[2 * ahead + 1 : 2 * ahead + 2, :] = jnp.where(lane + turn < 128, rows[1], rows[0])


def image_pairs(caption_partner_position, image_count):
    pairs = pl.pallas_call(
        pairs_kernel,
        out_shape=jax.ShapeDtypeStruct((image_count // 128, 128), jnp.int32),
        in_specs=[pl.BlockSpec(memory_space=pltpu.VMEM)],
        out_specs=pl.BlockSpec(memory_space=pltpu.VMEM),
        cost_estimate=pl.CostEstimate(flops=WAIT_FLOPS, bytes_accessed=0, transcendentals=0),
        compiler_params=pltpu.CompilerParams(vmem_limit_bytes=KERNEL_BYTES),
        name="pairs",
    )(caption_partner_position.reshape(-1, 128))
    return pairs.reshape(-1)


def scatter(parts, axes):
    count = lax.axis_size(axes)
    return lax.all_to_all(
        parts.reshape(count, parts.shape[0] // count, parts.shape[1]), axes, 0, 0, tiled=True
    )


def half(total):
    return total.astype(jnp.float16)


def full(total):
    return total.astype(jnp.float32)


def per_device(
    picture_vectors,
    caption_vectors,
    caption_partner_position,
    sharpness_factor,
    affine_offset_array,
):
    own_rows, width = picture_vectors.shape
    similarity_multiplier = sharpness_factor[0]
    shift = affine_offset_array[0]
    near_images = jnp.concatenate([picture_vectors, shift_by(picture_vectors, "ylo", 1)])
    near_images = normalize(near_images).astype(jnp.bfloat16)
    txt_block = gather(caption_vectors, TEXT_GROUP).reshape(-1, width)
    z_images = from_own(lax.all_gather(near_images, "z", axis=0, tiled=False), "z").reshape(-1, width)
    img_block = jnp.concatenate([z_images, shift_by(z_images, "core", 1)])
    image_count = img_block.shape[0]
    my_pairs = image_pairs(caption_partner_position, image_count)
    column = jnp.arange(txt_block.shape[0], dtype=jnp.int32)
    text_ids = (
        column // own_rows * image_count + lax.axis_index(IMAGE_GROUP) * own_rows + column % own_rows
    )
    logits = (
        similarity_multiplier
        * lax.dot_general(
            img_block, txt_block, (((1,), (1,)), ((), ())), preferred_element_type=jnp.float32
        )
        + shift
    )
    positive = (my_pairs[:, None] == text_ids[None, :]).astype(jnp.float32)
    sign = 2.0 * positive - 1.0
    loss = jnp.sum(jax.nn.softplus(-sign * logits), axis=1)
    slope = (jax.nn.sigmoid(logits) - positive).astype(jnp.bfloat16)
    txt_part = lax.dot_general(
        slope, img_block, (((0,), (0,)), ((), ())), preferred_element_type=jnp.float32
    )
    txt_terms = scatter(half(SEND_SCALE * txt_part), TEXT_GROUP)
    half_count = image_count // 2

    def image_part(rows):
        terms = SEND_SCALE * jnp.dot(slope[rows], txt_block, preferred_element_type=jnp.float32)
        losses = jnp.broadcast_to(loss[rows, None] * LOSS_SCALE, (half_count, 128))
        return jnp.concatenate([terms, losses], axis=1)

    came = shift_by(half(image_part(slice(half_count, image_count))), "core", 1)
    total = image_part(slice(0, half_count)) + full(came)
    total = total.reshape(8, 2 * own_rows, width + 128)
    far = shift_by(half(total[4]), "z", 4)
    ahead = full(shift_by(half(jnp.stack([total[1], total[3]])), "z", 1))
    back = full(shift_by(half(jnp.stack([total[7], total[5]])), "z", -1))
    near = total[0] + ahead[0] + back[0]
    near = near + full(shift_by(half(total[2] + ahead[1]), "z", 2))
    near = near + full(shift_by(half(total[6] + back[1]), "z", -2))
    near = near + full(far)
    total = near[:own_rows] + full(shift_by(half(near[own_rows:]), "ylo", 1))
    loss = total[:, width] / LOSS_SCALE
    img_dir = (similarity_multiplier / SEND_SCALE) * total[:, :width]
    txt_dir = (similarity_multiplier / SEND_SCALE) * jnp.sum(full(txt_terms), axis=0)
    unused, image_back = jax.vjp(normalize, picture_vectors.astype(jnp.float32))
    unused2, text_backward = jax.vjp(normalize, caption_vectors.astype(jnp.float32))
    return (image_back(img_dir)[0], text_backward(txt_dir)[0], loss)


def solution(mesh):
    fine = Mesh(mesh.devices.reshape(FINE_SIZES), FINE)
    in_specs = (P(FINE, None), P(FINE, None), P(), P(), P())
    out_specs = (P(FINE, None), P(FINE, None), P(FINE))
    return jax.shard_map(
        per_device, mesh=fine, in_specs=in_specs, out_specs=out_specs, check_vma=False
    )
```

```python
import jax
import jax.numpy as jnp
from jax import lax
from jax.experimental import pallas as pl
from jax.experimental.pallas import tpu as pltpu
from jax.sharding import Mesh, PartitionSpec as P

FINE = ("yhi", "x", "core", "z", "ylo")
FINE_SIZES = (4, 8, 2, 8, 2)
IMAGE_GROUP = ("core", "z", "ylo")
TEXT_GROUP = ("yhi", "x")
SEND_SCALE = 2.0
LOSS_SCALE = 0.125
WAIT_FLOPS = 100_000_000_000
KERNEL_BYTES = 4 * 1024 * 1024


def normalize(raw):
    values = raw.astype(jnp.float32)
    return values * lax.rsqrt(jnp.sum(values * values, axis=1, keepdims=True) + 1e-06)


def shift_by(block, axis, step):
    count = lax.axis_size(axis)
    return lax.ppermute(block, axis, [(i, (i + step) % count) for i in range(count)])


def from_own(array, axis):
    return lax.dynamic_slice_in_dim(
        jnp.concatenate([array, array]), lax.axis_index(axis), array.shape[0], 0
    )


def copies_kernel(raw_ref, copies_ref):
    rows = normalize(raw_ref[...]).astype(copies_ref.dtype)
    for place in range(copies_ref.shape[0]):
        copies_ref[place] = rows


def gather(raw, axes):
    copies = pl.pallas_call(
        copies_kernel,
        out_shape=jax.ShapeDtypeStruct((lax.axis_size(axes),) + raw.shape, jnp.bfloat16),
        in_specs=[pl.BlockSpec(memory_space=pltpu.VMEM)],
        out_specs=pl.BlockSpec(memory_space=pltpu.VMEM),
        compiler_params=pltpu.CompilerParams(vmem_limit_bytes=KERNEL_BYTES),
        name="copies",
    )(raw)
    return lax.all_to_all(copies, axes, 0, 0, tiled=True)


def pairs_kernel(all_ref, after_ref, *pairs_refs):
    group = lax.axis_index(TEXT_GROUP)
    core, z, ylo = [lax.axis_index(axis) for axis in IMAGE_GROUP]
    lane = lax.broadcasted_iota(jnp.int32, (1, 128), 1)
    turn = lax.rem(z, 4) * 32
    for ahead in range(2):
        first = group * 4 + lax.rem(core + ahead, 2) * 2
        rows = []
        for late in range(2):
            row = all_ref[pl.ds(first + lax.rem(z // 4 + late, 2), 1), :]
            swapped = jnp.where(lane % 32 < 16, pltpu.roll(row, 112, 1), pltpu.roll(row, 16, 1))
            rows.append(pltpu.roll(jnp.where(ylo == 0, row, swapped), lax.rem(128 - turn, 128), 1))
        pairs_refs[ahead][0:1, :] = jnp.where(lane + turn < 128, rows[0], rows[1])
        pairs_refs[ahead][1:2, :] = jnp.where(lane + turn < 128, rows[1], rows[0])


def image_pairs(caption_partner_position, core_images, after):
    pairs = pl.pallas_call(
        pairs_kernel,
        out_shape=[jax.ShapeDtypeStruct((core_images // 128, 128), jnp.int32)] * 2,
        in_specs=[pl.BlockSpec(memory_space=pltpu.VMEM), pl.BlockSpec(memory_space=pl.ANY)],
        out_specs=[pl.BlockSpec(memory_space=pltpu.VMEM)] * 2,
        cost_estimate=pl.CostEstimate(flops=WAIT_FLOPS, bytes_accessed=0, transcendentals=0),
        compiler_params=pltpu.CompilerParams(vmem_limit_bytes=KERNEL_BYTES),
        name="pairs",
    )(caption_partner_position.reshape(-1, 128), after)
    return [own_or_other.reshape(-1) for own_or_other in pairs]


def scatter(parts, axes):
    count = lax.axis_size(axes)
    return lax.all_to_all(
        parts.reshape(count, parts.shape[0] // count, parts.shape[1]), axes, 0, 0, tiled=True
    )


def half(total):
    return total.astype(jnp.float16)


def full(total):
    return total.astype(jnp.float32)


def per_device(
    picture_vectors,
    caption_vectors,
    caption_partner_position,
    sharpness_factor,
    affine_offset_array,
):
    own_rows, width = picture_vectors.shape
    similarity_multiplier = sharpness_factor[0]
    shift = affine_offset_array[0]
    near_images = jnp.concatenate([picture_vectors, shift_by(picture_vectors, "ylo", 1)])
    near_images = normalize(near_images).astype(jnp.bfloat16)
    txt_block = gather(caption_vectors, TEXT_GROUP).reshape(-1, width)
    z_images = from_own(lax.all_gather(near_images, "z", axis=0, tiled=False), "z").reshape(-1, width)
    other_images = shift_by(z_images, "core", 1)
    image_count = 2 * z_images.shape[0]
    own_pairs, other_pairs = image_pairs(caption_partner_position, image_count // 2, z_images[:16, :128])
    column = jnp.arange(txt_block.shape[0], dtype=jnp.int32)
    text_ids = (
        column // own_rows * image_count + lax.axis_index(IMAGE_GROUP) * own_rows + column % own_rows
    )

    def compare(images, partners):
        logits = (
            similarity_multiplier
            * lax.dot_general(
                images, txt_block, (((1,), (1,)), ((), ())), preferred_element_type=jnp.float32
            )
            + shift
        )
        positive = (partners[:, None] == text_ids[None, :]).astype(jnp.float32)
        sign = 2.0 * positive - 1.0
        loss = jnp.sum(jax.nn.softplus(-sign * logits), axis=1)
        return loss, (jax.nn.sigmoid(logits) - positive).astype(jnp.bfloat16)

    def image_part(loss, slope):
        terms = SEND_SCALE * jnp.dot(slope, txt_block, preferred_element_type=jnp.float32)
        losses = jnp.broadcast_to(loss[:, None] * LOSS_SCALE, (loss.shape[0], 128))
        return jnp.concatenate([terms, losses], axis=1)

    def text_part(slope, images):
        return lax.dot_general(
            slope, images, (((0,), (0,)), ((), ())), preferred_element_type=jnp.float32
        )

    own_loss, own_slope = compare(z_images, own_pairs)
    other_loss, other_slope = compare(other_images, other_pairs)
    txt_part = text_part(own_slope, z_images) + text_part(other_slope, other_images)
    txt_terms = scatter(half(SEND_SCALE * txt_part), TEXT_GROUP)
    came = shift_by(half(image_part(other_loss, other_slope)), "core", 1)
    total = image_part(own_loss, own_slope) + full(came)
    total = total.reshape(8, 2 * own_rows, width + 128)
    far = shift_by(half(total[4]), "z", 4)
    ahead = full(shift_by(half(jnp.stack([total[1], total[3]])), "z", 1))
    back = full(shift_by(half(jnp.stack([total[7], total[5]])), "z", -1))
    near = total[0] + ahead[0] + back[0]
    near = near + full(shift_by(half(total[2] + ahead[1]), "z", 2))
    near = near + full(shift_by(half(total[6] + back[1]), "z", -2))
    near = near + full(far)
    total = near[:own_rows] + full(shift_by(half(near[own_rows:]), "ylo", 1))
    loss = total[:, width] / LOSS_SCALE
    img_dir = (similarity_multiplier / SEND_SCALE) * total[:, :width]
    txt_dir = (similarity_multiplier / SEND_SCALE) * jnp.sum(full(txt_terms), axis=0)
    unused, image_back = jax.vjp(normalize, picture_vectors.astype(jnp.float32))
    unused2, text_backward = jax.vjp(normalize, caption_vectors.astype(jnp.float32))
    return (image_back(img_dir)[0], text_backward(txt_dir)[0], loss)


def solution(mesh):
    fine = Mesh(mesh.devices.reshape(FINE_SIZES), FINE)
    in_specs = (P(FINE, None), P(FINE, None), P(), P(), P())
    out_specs = (P(FINE, None), P(FINE, None), P(FINE))
    return jax.shard_map(
        per_device, mesh=fine, in_specs=in_specs, out_specs=out_specs, check_vma=False
    )
```

```python
import jax
import jax.numpy as jnp
from jax import lax
from jax.experimental import pallas as pl
from jax.experimental.pallas import tpu as pltpu
from jax.sharding import Mesh, PartitionSpec as P

FINE = ("yhi", "x", "core", "z", "ylo")
FINE_SIZES = (4, 8, 2, 8, 2)
IMAGE_GROUP = ("core", "z", "ylo")
TEXT_GROUP = ("yhi", "x")
SEND_SCALE = 2.0
LOSS_SCALE = 0.125
WAIT_FLOPS = 100_000_000_000
KERNEL_BYTES = 4 * 1024 * 1024


def normalize(raw):
    values = raw.astype(jnp.float32)
    return values * lax.rsqrt(jnp.sum(values * values, axis=1, keepdims=True) + 1e-06)


def shift_by(block, axis, step):
    count = lax.axis_size(axis)
    return lax.ppermute(block, axis, [(i, (i + step) % count) for i in range(count)])


def from_own(array, axis):
    return lax.dynamic_slice_in_dim(
        jnp.concatenate([array, array]), lax.axis_index(axis), array.shape[0], 0
    )


def copies_kernel(raw_ref, copies_ref):
    rows = normalize(raw_ref[...]).astype(copies_ref.dtype)
    for place in range(copies_ref.shape[0]):
        copies_ref[place] = rows


def gather(raw, axes):
    copies = pl.pallas_call(
        copies_kernel,
        out_shape=jax.ShapeDtypeStruct((lax.axis_size(axes),) + raw.shape, jnp.bfloat16),
        in_specs=[pl.BlockSpec(memory_space=pltpu.VMEM)],
        out_specs=pl.BlockSpec(memory_space=pltpu.VMEM),
        compiler_params=pltpu.CompilerParams(vmem_limit_bytes=KERNEL_BYTES),
        name="copies",
    )(raw)
    return lax.all_to_all(copies, axes, 0, 0, tiled=True)


def pairs_kernel(all_ref, after_ref, own_ref, other_ref, texts_ref):
    pairs_refs = (own_ref, other_ref)
    text = lax.broadcasted_iota(jnp.int32, texts_ref.shape, 0) * 128
    text = text + lax.broadcasted_iota(jnp.int32, texts_ref.shape, 1)
    owner_rows = own_ref.shape[0] * 2 * 128
    texts_ref[...] = text // 16 * owner_rows + lax.axis_index(IMAGE_GROUP) * 16 + text % 16
    group = lax.axis_index(TEXT_GROUP)
    core, z, ylo = [lax.axis_index(axis) for axis in IMAGE_GROUP]
    lane = lax.broadcasted_iota(jnp.int32, (1, 128), 1)
    turn = lax.rem(z, 4) * 32
    for ahead in range(2):
        first = group * 4 + lax.rem(core + ahead, 2) * 2
        rows = []
        for late in range(2):
            row = all_ref[pl.ds(first + lax.rem(z // 4 + late, 2), 1), :]
            swapped = jnp.where(lane % 32 < 16, pltpu.roll(row, 112, 1), pltpu.roll(row, 16, 1))
            rows.append(pltpu.roll(jnp.where(ylo == 0, row, swapped), lax.rem(128 - turn, 128), 1))
        pairs_refs[ahead][0:1, :] = jnp.where(lane + turn < 128, rows[0], rows[1])
        pairs_refs[ahead][1:2, :] = jnp.where(lane + turn < 128, rows[1], rows[0])


def image_pairs(caption_partner_position, core_images, text_count, after):
    pairs = pl.pallas_call(
        pairs_kernel,
        out_shape=[jax.ShapeDtypeStruct((core_images // 128, 128), jnp.int32)] * 2
        + [jax.ShapeDtypeStruct((text_count // 128, 128), jnp.int32)],
        in_specs=[pl.BlockSpec(memory_space=pltpu.VMEM), pl.BlockSpec(memory_space=pl.ANY)],
        out_specs=[pl.BlockSpec(memory_space=pltpu.VMEM)] * 3,
        cost_estimate=pl.CostEstimate(flops=WAIT_FLOPS, bytes_accessed=0, transcendentals=0),
        compiler_params=pltpu.CompilerParams(vmem_limit_bytes=KERNEL_BYTES),
        name="pairs",
    )(caption_partner_position.reshape(-1, 128), after)
    return [indices.reshape(-1) for indices in pairs]


def scatter(parts, axes):
    count = lax.axis_size(axes)
    return lax.all_to_all(
        parts.reshape(count, parts.shape[0] // count, parts.shape[1]), axes, 0, 0, tiled=True
    )


def half(total):
    return total.astype(jnp.float16)


def full(total):
    return total.astype(jnp.float32)


def per_device(
    picture_vectors,
    caption_vectors,
    caption_partner_position,
    sharpness_factor,
    affine_offset_array,
):
    own_rows, width = picture_vectors.shape
    similarity_multiplier = sharpness_factor[0]
    shift = affine_offset_array[0]
    near_images = jnp.concatenate([picture_vectors, shift_by(picture_vectors, "ylo", 1)])
    near_images = normalize(near_images).astype(jnp.bfloat16)
    txt_block = gather(caption_vectors, TEXT_GROUP).reshape(-1, width)
    z_images = from_own(lax.all_gather(near_images, "z", axis=0, tiled=False), "z").reshape(-1, width)
    other_images = shift_by(z_images, "core", 1)
    image_count = 2 * z_images.shape[0]
    own_pairs, other_pairs, text_ids = image_pairs(
        caption_partner_position, image_count // 2, txt_block.shape[0], z_images[:16, :128]
    )

    def compare(images, partners):
        logits = (
            similarity_multiplier
            * lax.dot_general(
                images, txt_block, (((1,), (1,)), ((), ())), preferred_element_type=jnp.float32
            )
            + shift
        )
        positive = (partners[:, None] == text_ids[None, :]).astype(jnp.float32)
        sign = 2.0 * positive - 1.0
        loss = jnp.sum(jax.nn.softplus(-sign * logits), axis=1)
        return loss, (jax.nn.sigmoid(logits) - positive).astype(jnp.bfloat16)

    def image_part(loss, slope):
        terms = SEND_SCALE * jnp.dot(slope, txt_block, preferred_element_type=jnp.float32)
        losses = jnp.broadcast_to(loss[:, None] * LOSS_SCALE, (loss.shape[0], 128))
        return jnp.concatenate([terms, losses], axis=1)

    def text_part(slope, images):
        return lax.dot_general(
            slope, images, (((0,), (0,)), ((), ())), preferred_element_type=jnp.float32
        )

    own_loss, own_slope = compare(z_images, own_pairs)
    other_loss, other_slope = compare(other_images, other_pairs)
    txt_part = text_part(own_slope, z_images) + text_part(other_slope, other_images)
    txt_terms = scatter(half(SEND_SCALE * txt_part), TEXT_GROUP)
    came = shift_by(half(image_part(other_loss, other_slope)), "core", 1)
    total = image_part(own_loss, own_slope) + full(came)
    total = total.reshape(8, 2 * own_rows, width + 128)
    far = shift_by(half(total[4]), "z", 4)
    ahead = full(shift_by(half(jnp.stack([total[1], total[3]])), "z", 1))
    back = full(shift_by(half(jnp.stack([total[7], total[5]])), "z", -1))
    near = total[0] + ahead[0] + back[0]
    near = near + full(shift_by(half(total[2] + ahead[1]), "z", 2))
    near = near + full(shift_by(half(total[6] + back[1]), "z", -2))
    near = near + full(far)
    total = near[:own_rows] + full(shift_by(half(near[own_rows:]), "ylo", 1))
    loss = total[:, width] / LOSS_SCALE
    img_dir = (similarity_multiplier / SEND_SCALE) * total[:, :width]
    txt_dir = (similarity_multiplier / SEND_SCALE) * jnp.sum(full(txt_terms), axis=0)
    unused, image_back = jax.vjp(normalize, picture_vectors.astype(jnp.float32))
    unused2, text_backward = jax.vjp(normalize, caption_vectors.astype(jnp.float32))
    return (image_back(img_dir)[0], text_backward(txt_dir)[0], loss)


def solution(mesh):
    fine = Mesh(mesh.devices.reshape(FINE_SIZES), FINE)
    in_specs = (P(FINE, None), P(FINE, None), P(), P(), P())
    out_specs = (P(FINE, None), P(FINE, None), P(FINE))
    return jax.shard_map(
        per_device, mesh=fine, in_specs=in_specs, out_specs=out_specs, check_vma=False
    )
```
